32 devices in a mesh: row: 8 (over y, x, core), col: 4 (over z).
Axes of the slice: x: 2, y: 2, z: 4, core: 2. Of those that a mesh axis runs over, the one named last changes fastest.
Arguments:
- values: bfloat16 [192, 24, 64, 64], P(('row', 'col')), may hold values from -6 to 6
- columns: int32 [192, 24], replicated, may hold values from 0 to 191, as said below
Outputs:
- purified: bfloat16 [192, 24, 64, 64], P(('row', 'col'))
The draws below stay inside these ranges and needn't reach their ends.
Inputs may be any that keep to these rules, and one draw needn't show every extreme that they name: Each block row i has 24 distinct block columns, each (i + o) modulo 192 with -12 <= o <= 12, in increasing order of o; the offsets -12 and 12 are always among them.
All inputs are finite; a program needn't handle non-finite values.
Results may differ from the reference program's by a relative error of at most 0.012.
Values may be sent and summed in bfloat16 or wider, within the bound.
A program may use at most 128 MiB of HBM per device.

```python
import math
import jax
import jax.numpy as jnp
from jax import lax

BS = 64
KNZ = 24
REACH = 12
ITERS = 1
NB = 192


def draw_columns(key, part):
    inner_count = 2 * REACH - 1
    row_keys = jax.random.split(key, NB)
    chosen = jax.vmap(lambda one_key: jax.random.permutation(one_key, inner_count))(row_keys)
    chosen = chosen[:, :KNZ - 2].astype(jnp.int32) - (REACH - 1)
    lower = jnp.full((NB, 1), -REACH, jnp.int32)
    upper = jnp.full((NB, 1), REACH, jnp.int32)
    offsets = jnp.sort(jnp.concatenate([lower, chosen, upper], axis=1), axis=1)
    row_ids = jnp.arange(NB, dtype=jnp.int32)[:, None]
    return ((row_ids + offsets) % NB).astype(jnp.int32)


def levels(stream_key, dims, cuts, smallest, top_value):
    def one(axis_at, shards_of):
        draws = jax.random.uniform(jax.random.fold_in(jax.random.fold_in(stream_key, 6), axis_at), (shards_of,), jnp.float32, smallest / len(cuts), top_value / len(cuts))
        return jnp.repeat(jnp.exp(draws), dims[axis_at] // shards_of).reshape((-1,) + (1,) * (len(dims) - axis_at - 1))

    level = one(*cuts[0])
    for cut in cuts[1:]:
        level = level * one(*cut)
    return level


def bell_draw(rng, extent, spread, reach, shards=(), held_as=jnp.bfloat16):
    array = spread * jax.random.normal(rng, extent, jnp.float32)
    if shards:
        array = array * levels(rng, extent, shards, -0.22, 0.18)
    return jnp.clip(array, -reach, reach).astype(held_as)


def setup_inputs(seed: int = 0) -> dict:
    arg_keys = jax.random.split(jax.random.key(seed), 3)
    return {
        "values": bell_draw(arg_keys[0], (NB, KNZ, BS, BS), 1.0, 6.0, ((0, 32),)),
        "columns": draw_columns(jax.random.fold_in(arg_keys[2], 71), 0),
    }


def filtered_product(left, right, columns, scale):
    knz = columns.shape[1]
    slot_ids = jnp.arange(knz, dtype=jnp.int32)

    def one_row(args):
        left_row, mine = args
        neighbour_cols = columns[mine]
        match = neighbour_cols[:, :, None] == mine[None, None, :]
        picked_slot = lax.optimization_barrier(jnp.sum(jnp.where(match, slot_ids[None, :, None], 0), axis=1)).astype(jnp.int32)
        present = jnp.any(match, axis=1)
        picked = right[mine[:, None], picked_slot]
        picked = jnp.where(present[:, :, None, None], picked.astype(jnp.float32), jnp.float32(0.0))
        product = jnp.einsum('axy,asyz->sxz', left_row.astype(jnp.float32), picked)
        return scale * product
    return lax.map(one_row, (left, columns), batch_size=16)

def reference(values, columns):
    scale = 0.6 / math.sqrt(KNZ * BS)
    current = values
    for step in range(ITERS):
        square = filtered_product(current, current, columns, scale).astype(jnp.bfloat16)
        cube = filtered_product(square, current, columns, scale)
        current = (3.0 * square.astype(jnp.float32) - 2.0 * cube).astype(jnp.bfloat16)
    return current
```

```python
import functools
import math

import jax
import jax.numpy as jnp
from jax import lax
from jax.experimental import pallas as pl
from jax.experimental.pallas import tpu as pltpu
from jax.sharding import PartitionSpec as P

REACH = 12
MESH = pl.DeviceIdType.MESH
OWN = -1
NEXT, PREV, NEXT2, PREV2 = 0, 1, 2, 3

NEED = {
    NEXT: lambda c: (0, 12 - c),
    PREV: lambda c: (2 - c, 12),
    NEXT2: lambda c: (0, 9 - c),
    PREV2: lambda c: (5 - c, 12),
}
MIRROR = {NEXT: PREV, PREV: NEXT, NEXT2: PREV2, PREV2: NEXT2, OWN: OWN}


def every(c):
    return (0, 12)


def relay_plan():
    down = {
        3: [(OWN, 0, 2, NEXT, every, 0)],
        2: [(OWN, 0, 1, NEXT, every, 0), (NEXT, 0, 1, NEXT2, every, 0)],
        1: [
            (OWN, 0, 0, NEXT, NEED[NEXT], 0),
            (NEXT, 0, 0, NEXT2, NEED[NEXT2], 0),
            (NEXT, 1, 0, PREV2, lambda c: (9 - c, 12), 0),
            (NEXT2, 1, 0, PREV, NEED[PREV], 0),
            (NEXT2, 1, 1, PREV2, NEED[PREV2], 0),
        ],
        0: [(NEXT2, 1, 0, PREV2, lambda c: (5 - c, 9 - c), 1)],
    }

    def flipped(pairs):
        def f(c):
            first, last = pairs(2 - c)
            return (12 - last, 12 - first)

        return f

    plan = {z: [] for z in range(4)}
    for z in range(4):
        a = down[z]
        b = [
            (MIRROR[s], -dl, 3 - dz, MIRROR[d], flipped(pairs), part)
            for s, dl, dz, d, pairs, part in down[3 - z]
        ]
        both = []
        for i in range(max(len(a), len(b))):
            both += a[i : i + 1] + b[i : i + 1]
        plan[z] = sorted(both, key=lambda t: t[0] != OWN)
    return plan


def kernel(n_rows, n_cols, values_ref, columns_ref, out_ref, pk, rx, rd, sq_ref, fin, send_sem, recv_sem):
    total = columns_ref.shape[0]
    row, col = lax.axis_index("row"), lax.axis_index("col")
    me = row * n_cols + col
    devices = n_rows * n_cols
    relay = n_cols == 4 and n_rows >= 3

    def place(linear):
        return (linear // n_cols, lax.rem(linear, n_cols))

    barrier = pltpu.get_barrier_semaphore()
    if relay:
        greeted = 0
        for dl in (-1, 0, 1):
            for dz in range(4):
                line = lax.rem(row + dl + n_rows, n_rows)
                other = lax.rem(col + dz, 4)
                if dl == 0 and dz == 0:
                    continue
                pl.semaphore_signal(barrier, inc=1, device_id=(line, other), device_id_type=MESH)
                greeted += 1
        pl.semaphore_wait(barrier, greeted)
    else:
        for step in (1, -1, 2, -2):
            other = place(lax.rem(me + step + devices, devices))
            pl.semaphore_signal(barrier, inc=1, device_id=other, device_id_type=MESH)
        pl.semaphore_wait(barrier, 4)

    for r in range(6):
        for p in range(12):
            pk[r, p] = jnp.concatenate([values_ref[r, 2 * p], values_ref[r, 2 * p + 1]], axis=1)

    def chunk(buffer, c, first, last):
        ref = pk if buffer == OWN else rx.at[buffer]
        return ref.at[pl.ds(2 * c, 2), pl.ds(first, last - first)]

    def describe(src, dst, pairs, part, c, sem, device):
        first, last = pairs(c)
        return pltpu.make_async_remote_copy(
            src_ref=chunk(src, c, first, last),
            dst_ref=chunk(dst, c, first, last),
            send_sem=send_sem.at[sem],
            recv_sem=recv_sem.at[dst, part, c],
            device_id=device,
            device_id_type=MESH,
        )

    lane = lax.broadcasted_iota(jnp.int32, (1, 128), 1)
    upper = (lane >= 64).astype(jnp.int32)
    slot = lax.broadcasted_iota(jnp.int32, (1, 24), 1)
    missing = []
    for k in range(30):
        block_row = lax.rem(me * 6 + (k - REACH) + total, total)
        found = columns_ref[pl.ds(block_row, 1), :]
        offset = found - block_row + REACH
        offset = jnp.where(offset < 0, offset + total, offset)
        offset = jnp.where(offset >= total, offset - total, offset)
        same = jnp.where(offset == slot, 1.0, 0.0)
        missing.append(jnp.sum(same, axis=1, keepdims=True).astype(jnp.int32))

    def build(k, read):
        m = missing[k]
        zero = jnp.zeros((64, 128), jnp.bfloat16)
        pair = lambda p: read(p) if 0 <= p < 12 else zero
        shifted = lambda p: jnp.concatenate([pair(p - 1)[:, 64:], pair(p)[:, :64]], axis=1)
        odd = k % 2
        base = (k - REACH + odd) // 2
        for q in range(15):
            p = q - base
            if p < -odd or p > 12 - odd:
                tile = zero
            else:
                w = 2 * p + odd + upper
                before = (w < m).astype(jnp.float32).astype(jnp.bfloat16)
                after = (w > m).astype(jnp.float32).astype(jnp.bfloat16)
                if odd:
                    tile = shifted(p + 1) * before + pair(p) * after
                else:
                    tile = pair(p) * before + shifted(p) * after
            rd[pl.ds(64 * k, 64), pl.ds(128 * q, 128)] = tile

    def run(transfers, incoming, target, meanwhile):
        here = set()
        started = []

        def arrive(dst, part, c, pairs):
            if (dst, part, c) in here:
                return
            here.add((dst, part, c))
            describe(OWN, dst, pairs, part, c, 0, target(0, 0)).wait_recv()

        pairs_of = {(dst, part): pairs for dst, part, pairs in incoming}
        done_own = False
        for src, dl, dz, dst, pairs, part in transfers:
            if src != OWN and not done_own:
                meanwhile()
                done_own = True
            for c in range(3):
                if src != OWN:
                    arrive(src, 0, c, pairs_of[(src, 0)])
                copy = describe(src, dst, pairs, part, c, len(started), target(dl, dz))
                copy.start()
                started.append(copy)
        if not done_own:
            meanwhile()
        for dst, part, pairs in incoming:
            for c in range(3):
                arrive(dst, part, c, pairs)
        return started

    def own_rows():
        for r in range(6):
            build(REACH + r, lambda p, r=r: pk[r, p])

    if relay:
        plan = relay_plan()
        for z in range(4):
            incoming = [
                (t[3], t[5], t[4]) for zz in range(4) for t in plan[zz] if t[2] == z
            ]

            @pl.when(col == z)
            def _(z=z, incoming=incoming):
                target = lambda dl, dz: (
                    lax.rem(row + dl + n_rows, n_rows),
                    jnp.int32(dz),
                )
                started = run(plan[z], incoming, target, lambda: None)
                for copy in started:
                    copy.wait_send()
        own_rows()
    else:
        steps = {NEXT: -1, PREV: 1, NEXT2: -2, PREV2: 2}
        transfers = [(OWN, s, 0, b, NEED[b], 0) for b, s in steps.items()]
        incoming = [(b, 0, NEED[b]) for b in steps]
        target = lambda s, _: place(lax.rem(me + s + devices, devices))
        started = run(transfers, incoming, target, own_rows)
        for copy in started:
            copy.wait_send()

    for buffer, first in ((NEXT, 18), (PREV, 6), (NEXT2, 24), (PREV2, 0)):
        for r in range(6):
            build(first + r, lambda p, b=buffer, r=r: rx[b, r, p])

    scale = 0.6 / math.sqrt(24 * 64)
    spans = [(0, 18), (0, 24), (0, 30), (6, 30), (12, 30)]
    wide = lax.broadcasted_iota(jnp.int32, (1, 384), 1) // 64
    for t, (k0, k1) in enumerate(spans):
        product = jnp.dot(
            rd[768:1152, 64 * k0 : 64 * k1],
            rd[64 * k0 : 64 * k1, 384 * t : 384 * t + 384],
            preferred_element_type=jnp.float32,
        )
        for r in range(6):
            w = wide + (6 * t - r)
            keep = (w >= 0) & (w <= 24) & (w != missing[REACH + r])
            part = product[64 * r : 64 * r + 64] * jnp.where(keep, scale, 0.0)
            sq_ref[64 * r : 64 * r + 64, 384 * t : 384 * t + 384] = part.astype(jnp.bfloat16)
    for t, (k0, k1) in enumerate(spans):
        product = jnp.dot(
            sq_ref[:, 64 * k0 : 64 * k1],
            rd[64 * k0 : 64 * k1, 384 * t : 384 * t + 384],
            preferred_element_type=jnp.float32,
        )
        square = sq_ref[:, 384 * t : 384 * t + 384].astype(jnp.float32)
        fin[:, 384 * t : 384 * t + 384] = 3.0 * square - (2.0 * scale) * product

    for r in range(6):
        m = missing[REACH + r]
        at = lambda c: fin[64 * r : 64 * r + 64, 64 * c : 64 * c + 64]
        for s in range(24):
            before = (s < m).astype(jnp.float32)
            out_ref[r, s] = (at(r + s) * before + at(r + s + 1) * (1.0 - before)).astype(jnp.bfloat16)


def shards(n_rows, n_cols, values, columns):
    return pl.pallas_call(
        functools.partial(kernel, n_rows, n_cols),
        out_shape=jax.ShapeDtypeStruct(values.shape, jnp.bfloat16),
        in_specs=[pl.BlockSpec(memory_space=pltpu.VMEM)] * 2,
        out_specs=pl.BlockSpec(memory_space=pltpu.VMEM),
        scratch_shapes=[
            pltpu.VMEM((6, 12, 64, 128), jnp.bfloat16),
            pltpu.VMEM((4, 6, 12, 64, 128), jnp.bfloat16),
            pltpu.VMEM((1920, 1920), jnp.bfloat16),
            pltpu.VMEM((384, 1920), jnp.bfloat16),
            pltpu.VMEM((384, 1920), jnp.float32),
            pltpu.SemaphoreType.DMA((32,)),
            pltpu.SemaphoreType.DMA((4, 2, 3)),
        ],
        compiler_params=pltpu.CompilerParams(
            collective_id=0, has_side_effects=True, vmem_limit_bytes=48 * 1024 * 1024
        ),
    )(values, columns)


def solution(mesh):
    placed = (P(("row", "col"), None, None, None), P())
    return jax.shard_map(
        functools.partial(shards, mesh.shape["row"], mesh.shape["col"]),
        mesh=mesh,
        in_specs=placed,
        out_specs=P(("row", "col"), None, None, None),
        check_vma=False,
    )
```

```python
import functools
import math

import jax
import jax.numpy as jnp
from jax import lax
from jax.experimental import pallas as pl
from jax.experimental.pallas import tpu as pltpu
from jax.sharding import PartitionSpec as P

REACH = 12
MESH = pl.DeviceIdType.MESH
OWN = -1
NEXT, PREV, NEXT2, PREV2 = 0, 1, 2, 3

NEED = {
    NEXT: lambda c: (0, 12 - c),
    PREV: lambda c: (2 - c, 12),
    NEXT2: lambda c: (0, 9 - c),
    PREV2: lambda c: (5 - c, 12),
}
MIRROR = {NEXT: PREV, PREV: NEXT, NEXT2: PREV2, PREV2: NEXT2, OWN: OWN}


def every(c):
    return (0, 12)


def relay_plan():
    down = {
        3: [(OWN, 0, 2, NEXT, every, 0)],
        2: [(OWN, 0, 1, NEXT, every, 0), (NEXT, 0, 1, NEXT2, every, 0)],
        1: [
            (OWN, 0, 0, NEXT, NEED[NEXT], 0),
            (NEXT, 0, 0, NEXT2, NEED[NEXT2], 0),
            (NEXT, 1, 0, PREV2, lambda c: (9 - c, 12), 0),
            (NEXT2, 1, 0, PREV, NEED[PREV], 0),
            (NEXT2, 1, 1, PREV2, NEED[PREV2], 0),
        ],
        0: [(NEXT2, 1, 0, PREV2, lambda c: (5 - c, 9 - c), 1)],
    }

    def flipped(pairs):
        def f(c):
            first, last = pairs(2 - c)
            return (12 - last, 12 - first)

        return f

    plan = {z: [] for z in range(4)}
    for z in range(4):
        a = down[z]
        b = [
            (MIRROR[s], -dl, 3 - dz, MIRROR[d], flipped(pairs), part)
            for s, dl, dz, d, pairs, part in down[3 - z]
        ]
        both = []
        for i in range(max(len(a), len(b))):
            both += a[i : i + 1] + b[i : i + 1]
        plan[z] = sorted(both, key=lambda t: t[0] != OWN)
    return plan


def kernel(
    n_rows, n_cols, values_ref, columns_ref, out_ref, vin, pk, rx, rd, sq_ref, fin, load_sem, send_sem, recv_sem
):
    total = columns_ref.shape[1]
    row, col = lax.axis_index("row"), lax.axis_index("col")
    me = row * n_cols + col
    devices = n_rows * n_cols
    relay = n_cols == 4 and n_rows >= 3

    def place(linear):
        return (linear // n_cols, lax.rem(linear, n_cols))

    loads = [
        pltpu.make_async_copy(
            values_ref.at[pl.ds(2 * c, 2)], vin.at[pl.ds(2 * c, 2)], load_sem.at[c]
        )
        for c in range(3)
    ]
    for load in loads:
        load.start()

    barrier = pltpu.get_barrier_semaphore()
    greeted = 0
    if relay:
        for dl in (-1, 0, 1):
            for dz in range(4):
                line = lax.rem(row + dl + n_rows, n_rows)
                other = lax.rem(col + dz, 4)
                if dl == 0 and dz == 0:
                    continue
                pl.semaphore_signal(barrier, inc=1, device_id=(line, other), device_id_type=MESH)
                greeted += 1
    else:
        for step in (1, -1, 2, -2):
            other = place(lax.rem(me + step + devices, devices))
            pl.semaphore_signal(barrier, inc=1, device_id=other, device_id_type=MESH)
            greeted += 1

    for c in range(3):
        loads[c].wait()
        for r in (2 * c, 2 * c + 1):
            for p in range(12):
                pk[r, p] = jnp.concatenate([vin[r, 2 * p], vin[r, 2 * p + 1]], axis=1)
    pl.semaphore_wait(barrier, greeted)

    def chunk(buffer, c, first, last):
        ref = pk if buffer == OWN else rx.at[buffer]
        return ref.at[pl.ds(2 * c, 2), pl.ds(first, last - first)]

    def describe(src, dst, pairs, part, c, sem, device):
        first, last = pairs(c)
        return pltpu.make_async_remote_copy(
            src_ref=chunk(src, c, first, last),
            dst_ref=chunk(dst, c, first, last),
            send_sem=send_sem.at[sem],
            recv_sem=recv_sem.at[dst, part, c],
            device_id=device,
            device_id_type=MESH,
        )

    class Place:
        def __init__(self, transfers, incoming, target):
            self.transfers, self.incoming, self.target = transfers, incoming, target
            self.here = set()
            self.started = []

        def arrive(self, dst, part, c):
            if (dst, part, c) not in self.here:
                self.here.add((dst, part, c))
                pairs = self.incoming[(dst, part)]
                describe(OWN, dst, pairs, part, c, 0, self.target(0, 0)).wait_recv()

        def arrive_chunk(self, dst, c):
            for d, part in self.incoming:
                if d == dst:
                    self.arrive(dst, part, c)

        def send(self, transfer):
            src, dl, dz, dst, pairs, part = transfer
            for c in range(3):
                if src != OWN:
                    self.arrive(src, 0, c)
                self.started.append((src, dst, pairs, part, c, len(self.started), dl, dz))
                self.copy(*self.started[-1]).start()

        def copy(self, src, dst, pairs, part, c, sem, dl, dz):
            return describe(src, dst, pairs, part, c, sem, self.target(dl, dz))

    if relay:
        plan = relay_plan()
        target = lambda dl, dz: (lax.rem(row + dl + n_rows, n_rows), col * 0 + dz)
        places = [
            Place(
                plan[z],
                {(t[3], t[5]): t[4] for zz in range(4) for t in plan[zz] if t[2] == z},
                target,
            )
            for z in range(4)
        ]
    else:
        steps = {NEXT: -1, PREV: 1, NEXT2: -2, PREV2: 2}
        target = lambda s, _: place(lax.rem(me + s + devices, devices))
        places = [
            Place(
                [(OWN, s, 0, b, NEED[b], 0) for b, s in steps.items()],
                {(b, 0): NEED[b] for b in steps},
                target,
            )
        ]

    def at_each_place(action, which=range(len(places))):
        for z in which:
            if len(places) == 1:
                action(places[z])
            else:

                @pl.when(col == z)
                def _(z=z):
                    action(places[z])

    def send_own(p):
        for t in p.transfers:
            if t[0] == OWN:
                p.send(t)

    at_each_place(send_own)

    lane = lax.broadcasted_iota(jnp.int32, (1, 128), 1)
    upper = (lane >= 64).astype(jnp.int32)
    found = columns_ref[...]
    rows_at = lax.broadcasted_iota(jnp.int32, found.shape, 1)
    offset = found - rows_at + REACH
    offset = jnp.where(offset < 0, offset + total, offset)
    offset = jnp.where(offset >= total, offset - total, offset)
    same = offset == lax.broadcasted_iota(jnp.int32, found.shape, 0)
    counts = jnp.sum(jnp.where(same, 1.0, 0.0), axis=0, keepdims=True)
    row_at = lax.broadcasted_iota(jnp.int32, (1, total), 1)
    missing = []
    for k in range(30):
        block_row = lax.rem(me * 6 + (k - REACH) + total, total)
        one = jnp.where(row_at == block_row, counts, 0.0)
        missing.append(jnp.sum(one, axis=1, keepdims=True).astype(jnp.int32))

    def build(k, read):
        m = missing[k]
        zero = jnp.zeros((64, 128), jnp.bfloat16)
        pair = lambda p: read(p) if 0 <= p < 12 else zero
        shifted = lambda p: jnp.concatenate([pair(p - 1)[:, 64:], pair(p)[:, :64]], axis=1)
        odd = k % 2
        base = (k - REACH + odd) // 2
        for q in range(15):
            p = q - base
            if p < -odd or p > 12 - odd:
                tile = zero
            else:
                w = 2 * p + odd + upper
                before = (w < m).astype(jnp.float32).astype(jnp.bfloat16)
                after = (w > m).astype(jnp.float32).astype(jnp.bfloat16)
                if odd:
                    tile = shifted(p + 1) * before + pair(p) * after
                else:
                    tile = pair(p) * before + shifted(p) * after
            rd[pl.ds(64 * k, 64), pl.ds(128 * q, 128)] = tile

    starts = {NEXT: 18, PREV: 6, NEXT2: 24, PREV2: 0}

    def build_received(buffer, r):
        build(starts[buffer] + r, lambda p: rx[buffer, r, p])

    for r in range(6):
        build(REACH + r, lambda p, r=r: pk[r, p])

    scale = 0.6 / math.sqrt(24 * 64)
    spans = [(0, 18), (0, 24), (0, 30), (6, 30), (12, 30)]
    wide = lax.broadcasted_iota(jnp.int32, (1, 384), 1) // 64

    def partial(left, t, ranges):
        result = None
        for k0, k1 in ranges:
            if k1 > k0:
                product = jnp.dot(
                    left(64 * k0, 64 * k1),
                    rd[64 * k0 : 64 * k1, 384 * t : 384 * t + 384],
                    preferred_element_type=jnp.float32,
                )
                result = product if result is None else result + product
        return result

    mine = lambda a, b: rd[768:1152, a:b]

    def squares(late, zs, wait_early, wait_late):
        at_each_place(wait_early, zs)
        for buffer in starts:
            if buffer != late:
                for r in range(6):
                    build_received(buffer, r)
        first, last = starts[late], starts[late] + 6
        for t, (k0, k1) in enumerate(spans):
            early = [(k0, min(k1, first)), (max(k0, last), k1)]
            fin[:, 384 * t : 384 * t + 384] = partial(mine, t, early)
        for c in range(3):
            at_each_place(lambda p: wait_late(p, c), zs)
            for r in (2 * c, 2 * c + 1):
                build_received(late, r)
        for t, (k0, k1) in enumerate(spans):
            product = fin[:, 384 * t : 384 * t + 384]
            more = partial(mine, t, [(max(k0, first), min(k1, last))])
            if more is not None:
                product = product + more
            for r in range(6):
                w = wide + (6 * t - r)
                keep = (w >= 0) & (w <= 24) & (w != missing[REACH + r])
                part = product[64 * r : 64 * r + 64] * jnp.where(keep, scale, 0.0)
                sq_ref[64 * r : 64 * r + 64, 384 * t : 384 * t + 384] = part.astype(jnp.bfloat16)

    def early_work(late):
        def work(p):
            for t in p.transfers:
                if t[0] != OWN:
                    p.send(t)
            for c in range(3):
                for dst in starts:
                    if dst != late:
                        p.arrive_chunk(dst, c)

        return work

    def late_work(late):
        return lambda p, c: p.arrive_chunk(late, c)

    if relay:

        @pl.when(col < 2)
        def _():
            squares(PREV, (0, 1), early_work(PREV), late_work(PREV))

        @pl.when(col >= 2)
        def _():
            squares(NEXT, (2, 3), early_work(NEXT), late_work(NEXT))
    else:
        squares(PREV, (0,), early_work(PREV), late_work(PREV))

    for t, (k0, k1) in enumerate(spans):
        product = partial(lambda a, b: sq_ref[:, a:b], t, [(k0, k1)])
        square = sq_ref[:, 384 * t : 384 * t + 384].astype(jnp.float32)
        fin[:, 384 * t : 384 * t + 384] = 3.0 * square - (2.0 * scale) * product

    for r in range(6):
        m = missing[REACH + r]
        at = lambda c: fin[64 * r : 64 * r + 64, 64 * c : 64 * c + 64]
        for s in range(24):
            before = (s < m).astype(jnp.float32)
            out_ref[r, s] = (at(r + s) * before + at(r + s + 1) * (1.0 - before)).astype(jnp.bfloat16)

    def drain(p):
        for sent in p.started:
            p.copy(*sent).wait_send()

    at_each_place(drain)


def shards(n_rows, n_cols, values, columns):
    return pl.pallas_call(
        functools.partial(kernel, n_rows, n_cols),
        out_shape=jax.ShapeDtypeStruct(values.shape, jnp.bfloat16),
        in_specs=[pl.BlockSpec(memory_space=pl.ANY), pl.BlockSpec(memory_space=pltpu.VMEM)],
        out_specs=pl.BlockSpec(memory_space=pltpu.VMEM),
        scratch_shapes=[
            pltpu.VMEM(values.shape, jnp.bfloat16),
            pltpu.VMEM((6, 12, 64, 128), jnp.bfloat16),
            pltpu.VMEM((4, 6, 12, 64, 128), jnp.bfloat16),
            pltpu.VMEM((1920, 1920), jnp.bfloat16),
            pltpu.VMEM((384, 1920), jnp.bfloat16),
            pltpu.VMEM((384, 1920), jnp.float32),
            pltpu.SemaphoreType.DMA((3,)),
            pltpu.SemaphoreType.DMA((32,)),
            pltpu.SemaphoreType.DMA((4, 2, 3)),
        ],
        compiler_params=pltpu.CompilerParams(
            collective_id=0, has_side_effects=True, vmem_limit_bytes=60 * 1024 * 1024
        ),
    )(values, columns.T)


def solution(mesh):
    placed = (P(("row", "col"), None, None, None), P())
    return jax.shard_map(
        functools.partial(shards, mesh.shape["row"], mesh.shape["col"]),
        mesh=mesh,
        in_specs=placed,
        out_specs=P(("row", "col"), None, None, None),
        check_vma=False,
    )
```

```python
import functools
import math

import jax
import jax.numpy as jnp
from jax import lax
from jax.experimental import pallas as pl
from jax.experimental.pallas import tpu as pltpu
from jax.sharding import PartitionSpec as P

REACH = 12
MESH = pl.DeviceIdType.MESH
OWN = -1
NEXT, PREV, NEXT2, PREV2 = 0, 1, 2, 3

NEED = {
    NEXT: lambda c: (0, 12 - c),
    PREV: lambda c: (2 - c, 12),
    NEXT2: lambda c: (0, 9 - c),
    PREV2: lambda c: (5 - c, 12),
}
MIRROR = {NEXT: PREV, PREV: NEXT, NEXT2: PREV2, PREV2: NEXT2, OWN: OWN}


def every(c):
    return (0, 12)


def relay_plan():
    down = {
        3: [(OWN, 0, 2, NEXT, every, 0)],
        2: [(OWN, 0, 1, NEXT, every, 0), (NEXT, 0, 1, NEXT2, every, 0)],
        1: [
            (OWN, 0, 0, NEXT, NEED[NEXT], 0),
            (NEXT, 0, 0, NEXT2, NEED[NEXT2], 0),
            (NEXT, 1, 0, PREV2, lambda c: (9 - c, 12), 0),
            (NEXT2, 1, 0, PREV, NEED[PREV], 0),
            (NEXT2, 1, 1, PREV2, NEED[PREV2], 0),
        ],
        0: [(NEXT2, 1, 0, PREV2, lambda c: (5 - c, 9 - c), 1)],
    }

    def flipped(pairs):
        def f(c):
            first, last = pairs(2 - c)
            return (12 - last, 12 - first)

        return f

    plan = {z: [] for z in range(4)}
    for z in range(4):
        a = down[z]
        b = [
            (MIRROR[s], -dl, 3 - dz, MIRROR[d], flipped(pairs), part)
            for s, dl, dz, d, pairs, part in down[3 - z]
        ]
        both = []
        for i in range(max(len(a), len(b))):
            both += a[i : i + 1] + b[i : i + 1]
        plan[z] = sorted(both, key=lambda t: t[0] != OWN)
    return plan


def kernel(
    n_rows, n_cols, values_ref, columns_ref, out_ref, vin, pk, rx, rd, sq_ref, fin, band, load_sem, send_sem, recv_sem
):
    total = columns_ref.shape[1]
    row, col = lax.axis_index("row"), lax.axis_index("col")
    me = row * n_cols + col
    devices = n_rows * n_cols
    relay = n_cols == 4 and n_rows >= 3

    def place(linear):
        return (linear // n_cols, lax.rem(linear, n_cols))

    loads = [
        pltpu.make_async_copy(
            values_ref.at[pl.ds(2 * c, 2)], vin.at[pl.ds(2 * c, 2)], load_sem.at[c]
        )
        for c in range(3)
    ]
    for load in loads:
        load.start()

    barrier = pltpu.get_barrier_semaphore()
    greeted = 0
    if relay:
        for dl in (-1, 0, 1):
            for dz in range(4):
                line = lax.rem(row + dl + n_rows, n_rows)
                other = lax.rem(col + dz, 4)
                if dl == 0 and dz == 0:
                    continue
                pl.semaphore_signal(barrier, inc=1, device_id=(line, other), device_id_type=MESH)
                greeted += 1
    else:
        for step in (1, -1, 2, -2):
            other = place(lax.rem(me + step + devices, devices))
            pl.semaphore_signal(barrier, inc=1, device_id=other, device_id_type=MESH)
            greeted += 1

    for c in range(3):
        loads[c].wait()
        for r in (2 * c, 2 * c + 1):
            for p in range(12):
                pk[r, p] = jnp.concatenate([vin[r, 2 * p], vin[r, 2 * p + 1]], axis=1)
    pl.semaphore_wait(barrier, greeted)

    def chunk(buffer, c, first, last):
        ref = pk if buffer == OWN else rx.at[buffer]
        return ref.at[pl.ds(2 * c, 2), pl.ds(first, last - first)]

    def describe(src, dst, pairs, part, c, sem, device):
        first, last = pairs(c)
        return pltpu.make_async_remote_copy(
            src_ref=chunk(src, c, first, last),
            dst_ref=chunk(dst, c, first, last),
            send_sem=send_sem.at[sem],
            recv_sem=recv_sem.at[dst, part, c],
            device_id=device,
            device_id_type=MESH,
        )

    class Place:
        def __init__(self, transfers, incoming, target):
            self.transfers, self.incoming, self.target = transfers, incoming, target
            self.here = set()
            self.started = []

        def arrive(self, dst, part, c):
            if (dst, part, c) not in self.here:
                self.here.add((dst, part, c))
                pairs = self.incoming[(dst, part)]
                describe(OWN, dst, pairs, part, c, 0, self.target(0, 0)).wait_recv()

        def arrive_chunk(self, dst, c):
            for d, part in self.incoming:
                if d == dst:
                    self.arrive(dst, part, c)

        def send(self, transfer):
            src, dl, dz, dst, pairs, part = transfer
            for c in range(3):
                if src != OWN:
                    self.arrive(src, 0, c)
                self.started.append((src, dst, pairs, part, c, len(self.started), dl, dz))
                self.copy(*self.started[-1]).start()

        def copy(self, src, dst, pairs, part, c, sem, dl, dz):
            return describe(src, dst, pairs, part, c, sem, self.target(dl, dz))

    if relay:
        plan = relay_plan()
        target = lambda dl, dz: (lax.rem(row + dl + n_rows, n_rows), col * 0 + dz)
        places = [
            Place(
                plan[z],
                {(t[3], t[5]): t[4] for zz in range(4) for t in plan[zz] if t[2] == z},
                target,
            )
            for z in range(4)
        ]
    else:
        steps = {NEXT: -1, PREV: 1, NEXT2: -2, PREV2: 2}
        target = lambda s, _: place(lax.rem(me + s + devices, devices))
        places = [
            Place(
                [(OWN, s, 0, b, NEED[b], 0) for b, s in steps.items()],
                {(b, 0): NEED[b] for b in steps},
                target,
            )
        ]

    def at_each_place(action, which=range(len(places))):
        for z in which:
            if len(places) == 1:
                action(places[z])
            else:

                @pl.when(col == z)
                def _(z=z):
                    action(places[z])

    def send_own(p):
        for t in p.transfers:
            if t[0] == OWN:
                p.send(t)

    at_each_place(send_own)

    lane = lax.broadcasted_iota(jnp.int32, (1, 128), 1)
    upper = (lane >= 64).astype(jnp.int32)
    found = columns_ref[...]
    rows_at = lax.broadcasted_iota(jnp.int32, found.shape, 1)
    offset = found - rows_at + REACH
    offset = jnp.where(offset < 0, offset + total, offset)
    offset = jnp.where(offset >= total, offset - total, offset)
    same = offset == lax.broadcasted_iota(jnp.int32, found.shape, 0)
    counts = jnp.sum(jnp.where(same, 1.0, 0.0), axis=0, keepdims=True)
    row_at = lax.broadcasted_iota(jnp.int32, (1, total), 1)
    missing = []
    for k in range(30):
        block_row = lax.rem(me * 6 + (k - REACH) + total, total)
        one = jnp.where(row_at == block_row, counts, 0.0)
        missing.append(jnp.sum(one, axis=1, keepdims=True).astype(jnp.int32))

    def build(k, read):
        m = missing[k]
        zero = jnp.zeros((64, 128), jnp.bfloat16)
        pair = lambda p: read(p) if 0 <= p < 12 else zero
        shifted = lambda p: jnp.concatenate([pair(p - 1)[:, 64:], pair(p)[:, :64]], axis=1)
        odd = k % 2
        base = (k - REACH + odd) // 2
        for q in range(15):
            p = q - base
            if p < -odd or p > 12 - odd:
                tile = zero
            else:
                w = 2 * p + odd + upper
                before = (w < m).astype(jnp.float32).astype(jnp.bfloat16)
                after = (w > m).astype(jnp.float32).astype(jnp.bfloat16)
                if odd:
                    tile = shifted(p + 1) * before + pair(p) * after
                else:
                    tile = pair(p) * before + shifted(p) * after
            rd[pl.ds(64 * k, 64), pl.ds(128 * q, 128)] = tile

    starts = {NEXT: 18, PREV: 6, NEXT2: 24, PREV2: 0}

    def build_received(buffer, r):
        build(starts[buffer] + r, lambda p: rx[buffer, r, p])

    for r in range(6):
        build(REACH + r, lambda p, r=r: pk[r, p])

    scale = 0.6 / math.sqrt(24 * 64)
    tiles = [(c, min(c + 4, 30)) for c in range(0, 30, 4)]
    spans = [(max(0, c0 - REACH), min(30, c1 + REACH)) for c0, c1 in tiles]
    wide = lax.broadcasted_iota(jnp.int32, (1, 256), 1) // 64
    lanes = lambda t: slice(64 * tiles[t][0], 64 * tiles[t][1])

    def partial(left, t, ranges):
        result = None
        for k0, k1 in ranges:
            if k1 > k0:
                product = jnp.dot(
                    left(64 * k0, 64 * k1),
                    rd[64 * k0 : 64 * k1, lanes(t)],
                    preferred_element_type=jnp.float32,
                )
                result = product if result is None else result + product
        return result

    mine = lambda a, b: rd[768:1152, a:b]

    def squares(late, zs, wait_early, wait_late):
        at_each_place(wait_early, zs)
        for buffer in starts:
            if buffer != late:
                for r in range(6):
                    build_received(buffer, r)
        first, last = starts[late], starts[late] + 6
        for t, (k0, k1) in enumerate(spans):
            early = [(k0, min(k1, first)), (max(k0, last), k1)]
            fin[:, lanes(t)] = partial(mine, t, early)
        for c in range(3):
            at_each_place(lambda p: wait_late(p, c), zs)
            for r in (2 * c, 2 * c + 1):
                build_received(late, r)
        for t, (k0, k1) in enumerate(spans):
            product = fin[:, lanes(t)]
            more = partial(mine, t, [(max(k0, first), min(k1, last))])
            if more is not None:
                product = product + more
            for r in range(6):
                w = wide[:, : 64 * (tiles[t][1] - tiles[t][0])] + (tiles[t][0] - r)
                keep = (w >= 0) & (w <= 24) & (w != missing[REACH + r])
                part = product[64 * r : 64 * r + 64] * jnp.where(keep, scale, 0.0)
                sq_ref[64 * r : 64 * r + 64, lanes(t)] = part.astype(jnp.bfloat16)

    def early_work(late):
        def work(p):
            for t in p.transfers:
                if t[0] != OWN:
                    p.send(t)
            for c in range(3):
                for dst in starts:
                    if dst != late:
                        p.arrive_chunk(dst, c)

        return work

    def late_work(late):
        return lambda p, c: p.arrive_chunk(late, c)

    if relay:

        @pl.when(col < 2)
        def _():
            squares(PREV, (0, 1), early_work(PREV), late_work(PREV))

        @pl.when(col >= 2)
        def _():
            squares(NEXT, (2, 3), early_work(NEXT), late_work(NEXT))
    else:
        squares(PREV, (0,), early_work(PREV), late_work(PREV))

    for t, (k0, k1) in enumerate(spans):
        product = partial(lambda a, b: sq_ref[:, a:b], t, [(k0, k1)])
        square = sq_ref[:, lanes(t)].astype(jnp.float32)
        band[:, lanes(t)] = (3.0 * square - (2.0 * scale) * product).astype(jnp.bfloat16)

    for r in range(6):
        m = missing[REACH + r]
        at = lambda c: band[64 * r : 64 * r + 64, 64 * c : 64 * c + 64]
        for s in range(24):
            here = (lane[:, :64] * 0 + s) < m
            before = here.astype(jnp.float32).astype(jnp.bfloat16)
            after = 1.0 - here.astype(jnp.float32)
            out_ref[r, s] = at(r + s) * before + at(r + s + 1) * after.astype(jnp.bfloat16)

    def drain(p):
        for sent in p.started:
            p.copy(*sent).wait_send()

    at_each_place(drain)


def shards(n_rows, n_cols, values, columns):
    return pl.pallas_call(
        functools.partial(kernel, n_rows, n_cols),
        out_shape=jax.ShapeDtypeStruct(values.shape, jnp.bfloat16),
        in_specs=[pl.BlockSpec(memory_space=pltpu.HBM), pl.BlockSpec(memory_space=pltpu.VMEM)],
        out_specs=pl.BlockSpec(memory_space=pltpu.VMEM),
        scratch_shapes=[
            pltpu.VMEM(values.shape, jnp.bfloat16),
            pltpu.VMEM((6, 12, 64, 128), jnp.bfloat16),
            pltpu.VMEM((4, 6, 12, 64, 128), jnp.bfloat16),
            pltpu.VMEM((1920, 1920), jnp.bfloat16),
            pltpu.VMEM((384, 1920), jnp.bfloat16),
            pltpu.VMEM((384, 1920), jnp.float32),
            pltpu.VMEM((384, 1920), jnp.bfloat16),
            pltpu.SemaphoreType.DMA((3,)),
            pltpu.SemaphoreType.DMA((32,)),
            pltpu.SemaphoreType.DMA((4, 2, 3)),
        ],
        compiler_params=pltpu.CompilerParams(
            collective_id=0, has_side_effects=True, vmem_limit_bytes=48 * 1024 * 1024
        ),
    )(values, columns.T)


def solution(mesh):
    placed = (P(("row", "col"), None, None, None), P())
    return jax.shard_map(
        functools.partial(shards, mesh.shape["row"], mesh.shape["col"]),
        mesh=mesh,
        in_specs=placed,
        out_specs=P(("row", "col"), None, None, None),
        check_vma=False,
    )
```
